32 devices in a mesh: cl: 8 (over z, y), rep: 4 (over x, core).
Axes of the slice: x: 2, y: 2, z: 4, core: 2. Of those that a mesh axis runs over, the one named last changes fastest.
Arguments:
- points: float32 [3, 8192], P(None, 'cl'), as said below
- sketch: bfloat16 [64, 8192], P(None, 'cl'), may hold values from -6 to 6
- send_ids: int32 [8, 4, 8, 1], P('cl', 'rep'), may hold values from 0 to 3
- tile_order: int32 [8, 4, 8], P('cl', 'rep'), may hold values from 0 to 7, as said below
- tile_rows: int32 [8, 4, 8], P('cl', 'rep'), may hold values from 0 to 3, as said below
- tile_count: int32 [8, 4], P('cl', 'rep'), may hold values from 1 to 8, as said below
Outputs:
- sketch_sum: float32 [2, 64, 8192], P(None, None, ('cl', 'rep'))
- gram: float32 [32, 128, 128], P(('cl', 'rep'))
The draws below stay inside these ranges and needn't reach their ends.
Inputs may be any that keep to these rules, and one draw needn't show every extreme that they name: Each cluster's points lie in its own box; points of distinct clusters are at least 1 apart. `tile_order`: for each device, a permutation of its 8 slots. `tile_rows`: A list entry's row cluster is never its column cluster. `tile_count`: some device has all 8 entries admissible.
All inputs are finite; a program needn't handle non-finite values.
Results may differ from the reference program's by a relative error of at most 0.003.
Values may be sent and summed in bfloat16 or wider, within the bound.
A program may use at most 64 MiB of HBM per device.

```python
import math
import jax
import jax.numpy as jnp
from jax import lax

CLUSTER = 256
SK = 64
CL_DEV = 4
CAP = 1
SLOTS = 8
CLUSTERS = 32
NPTS = 8192
N_CL = 8
N_REP = 4


def plan_lists(key):
    send_key = jax.random.fold_in(key, 101)
    order_key = jax.random.fold_in(key, 102)
    row_key = jax.random.fold_in(key, 103)
    shift_key = jax.random.fold_in(key, 104)
    send_ids = jax.random.randint(send_key, (N_CL, N_REP, N_CL, CAP), 0, CL_DEV, dtype=jnp.int32)
    order_keys = jax.random.split(order_key, N_CL * N_REP)
    tile_order = jax.vmap(lambda single: jax.random.permutation(single, SLOTS))(order_keys)
    tile_order = tile_order.reshape(N_CL, N_REP, SLOTS).astype(jnp.int32)
    owner = jnp.arange(N_CL, dtype=jnp.int32)[:, None, None]
    replica = jnp.arange(N_REP, dtype=jnp.int32)[None, :, None]
    source = tile_order // CAP
    within = tile_order % CAP
    column_local = send_ids[source, replica, owner, within]
    loose = jax.random.randint(row_key, (N_CL, N_REP, SLOTS), 0, CL_DEV, dtype=jnp.int32)
    offset_draw = jax.random.randint(shift_key, (N_CL, N_REP, SLOTS), 0, CL_DEV - 1, dtype=jnp.int32)
    avoided = (column_local + 1 + offset_draw) % CL_DEV
    tile_rows = jnp.where(source == owner, avoided, loose).astype(jnp.int32)
    return (send_ids, tile_order, tile_rows)


def draw_send_ids(key, part):
    return plan_lists(key)[0]


def draw_tile_order(key, part):
    return plan_lists(key)[1]


def draw_tile_rows(key, part):
    return plan_lists(key)[2]


def draw_tile_count(key, part):
    key = jax.random.fold_in(key, 7)
    light_key = jax.random.fold_in(key, 1)
    heavy_key = jax.random.fold_in(key, 2)
    pick_key = jax.random.fold_in(key, 3)
    light = jax.random.randint(light_key, (N_CL, N_REP), 1, SLOTS // 2 + 1, dtype=jnp.int32)
    heavy = jax.random.randint(heavy_key, (N_CL, N_REP), 0, 8, dtype=jnp.int32) == 0
    chosen = jax.random.randint(pick_key, (), 0, N_CL * N_REP, dtype=jnp.int32)
    flat_index = jnp.arange(N_CL * N_REP, dtype=jnp.int32).reshape(N_CL, N_REP)
    return jnp.where(heavy | (flat_index == chosen), SLOTS, light).astype(jnp.int32)


def draw_points(key, part):
    key = jax.random.fold_in(key, 5)
    cluster_ids = jnp.arange(CLUSTERS, dtype=jnp.int32)
    boxes = []
    for coord in range(3):
        value = jnp.zeros((CLUSTERS,), jnp.int32)
        for digit in range(8):
            value = value + ((cluster_ids >> 3 * digit + coord & 1) << digit)
        boxes.append(value)
    corner = 2.0 * jnp.stack(boxes).astype(jnp.float32)
    spread = jax.random.uniform(key, (3, CLUSTERS, CLUSTER), jnp.float32)
    return (corner[:, :, None] + spread).reshape(3, NPTS)


def level_of(rng, dims, cuts, least, top_value):
    def one(position, blocks):
        steps = jax.random.uniform(jax.random.fold_in(jax.random.fold_in(rng, 6), position), (blocks,), jnp.float32, least / len(cuts), top_value / len(cuts))
        return jnp.repeat(jnp.exp(steps), dims[position] // blocks).reshape((-1,) + (1,) * (len(dims) - position - 1))

    factor_of = one(*cuts[0])
    for cut in cuts[1:]:
        factor_of = factor_of * one(*cut)
    return factor_of


def normal_values(key, dims, scale, reach, cuts=(), held_as=jnp.bfloat16):
    values = jax.random.normal(key, dims, jnp.float32) * scale
    if len(cuts) > 0:
        values = level_of(key, dims, cuts, -0.22, 0.18) * values
    return jnp.clip(values, min=-reach, max=reach).astype(held_as)


def setup_inputs(seed: int = 0) -> dict:
    splits = jax.random.split(jax.random.key(seed), 7)
    points = draw_points(jax.random.fold_in(splits[6], 71), 0)
    sketch = normal_values(splits[1], (SK, NPTS), 1.0, 6.0, ((1, 8),))
    send_ids = draw_send_ids(jax.random.fold_in(splits[6], 71), 0)
    tile_order = draw_tile_order(jax.random.fold_in(splits[6], 71), 0)
    tile_rows = draw_tile_rows(jax.random.fold_in(splits[6], 71), 0)
    tile_count = draw_tile_count(jax.random.fold_in(splits[6], 71), 0)
    return {"points": points, "sketch": sketch, "send_ids": send_ids, "tile_order": tile_order, "tile_rows": tile_rows, "tile_count": tile_count}


WAVENUMBER = 16.0
INV_FOUR_PI = 1.0 / (4.0 * math.pi)

def tile_kernel(col_coords, row_coords):
    squared = jnp.zeros((col_coords.shape[1], col_coords.shape[2], row_coords.shape[2]), jnp.float32)
    for coord in range(3):
        differ = col_coords[coord][:, :, None] - row_coords[coord][:, None, :]
        squared = squared + differ * differ
    distance = jnp.sqrt(squared)
    phase_arg = WAVENUMBER * distance
    inverse = INV_FOUR_PI / distance
    real_part = (jnp.cos(phase_arg) * inverse).astype(jnp.bfloat16)
    imag_part = (jnp.sin(phase_arg) * inverse).astype(jnp.bfloat16)
    return (real_part, imag_part)

def reference(points, sketch, send_ids, tile_order, tile_rows, tile_count):
    coords = points.reshape(3, CLUSTERS, CLUSTER)
    sketches = sketch.reshape(SK, CLUSTERS, CLUSTER)
    owner = jnp.arange(N_CL, dtype=jnp.int32)[:, None, None]
    replica = jnp.arange(N_REP, dtype=jnp.int32)[None, :, None]
    source = tile_order // CAP
    within = tile_order % CAP
    col_ids = (source * CL_DEV + send_ids[source, replica, owner, within]).astype(jnp.int32)
    row_ids = (owner * CL_DEV + tile_rows).astype(jnp.int32)
    active = jnp.arange(SLOTS, dtype=jnp.int32)[None, None, :] < tile_count[:, :, None]
    col_ids = col_ids.reshape(-1, 8)
    row_ids = row_ids.reshape(-1, 8)
    active = active.reshape(-1, 8)

    def advance(carry, pieces):
        col_part, row_part, active_part = pieces

        def compute(inner):
            real_part, imag_part = tile_kernel(coords[:, col_part], coords[:, row_part])
            weights = jnp.where(active_part[None, :, None], sketches[:, col_part], jnp.zeros_like(sketches[:, col_part]))
            weights = weights.astype(jnp.float32)
            real_term = jnp.einsum('sbc,bcr->bsr', weights, real_part.astype(jnp.float32))
            imag_term = jnp.einsum('sbc,bcr->bsr', weights, imag_part.astype(jnp.float32))
            terms = jnp.stack([real_term, imag_term], axis=1)
            return inner.at[row_part].add(terms)

        def unchanged(inner):
            return inner
        return (lax.cond(jnp.any(active_part), compute, unchanged, carry), None)
    start_sum = jnp.zeros((CLUSTERS, 2, SK, CLUSTER), jnp.float32)
    summed = lax.scan(advance, start_sum, (col_ids, row_ids, active))[0]
    sketch_sum = summed.transpose(1, 2, 0, 3).reshape(2, SK, NPTS)
    matrix = summed.reshape(CLUSTERS, 2 * SK, CLUSTER)
    gram = jnp.einsum('lac,lbc->lab', matrix, matrix, precision=lax.Precision.HIGHEST) / CLUSTER
    return (sketch_sum, gram)
```

```python
import functools
import math

import jax
import jax.numpy as jnp
from jax import lax
from jax.experimental import pallas as pl
from jax.experimental.pallas import tpu as pltpu
from jax.sharding import PartitionSpec as P

CLUSTER = 256
SK = 64
WAVENUMBER = 16.0
INV_FOUR_PI = 1.0 / (4.0 * math.pi)
TURNS = WAVENUMBER / (2.0 * math.pi)
MESH = pl.DeviceIdType.MESH

def _fit(fun, terms):
    import numpy as np

    nodes = (np.cos((np.arange(64) + 0.5) * np.pi / 64) + 1.0) / 8.0
    return [float(c) for c in np.polynomial.chebyshev.Chebyshev.fit(
        nodes, fun(np.sqrt(nodes)), terms - 1, domain=[0.0, 0.25]
    ).convert(kind=np.polynomial.Polynomial).coef]


def _coefficients():
    import numpy as np

    root = math.sqrt(2.0)
    return (
        _fit(lambda r: root * np.sin(np.pi * r) / r, 5),
        _fit(lambda r: root * np.cos(np.pi * r), 5),
    )


SIN_C, COS_C = _coefficients()


def horner(coefs, u):
    value = coefs[-1]
    for c in coefs[-2::-1]:
        value = value * u + c
    return value


def xor(index, mask):
    bit, result = 1, index
    while bit <= mask:
        if mask & bit:
            result = result + bit * (1 - 2 * ((index // bit) % 2))
        bit *= 2
    return result


def kernel(
    n_cl, n_rep,
    send_ids, order, rows, count, points_hbm, sketch_hbm,
    out_ref, gram_ref,
    pts, skt, send_c, send_s, recv_c, recv_s, row_b, tile_re, tile_im, acc, rs_send, rs_recv,
    local_sem, csend, crecv, ssend, srecv, rsend, rrecv,
):
    me = lax.axis_index("cl")
    my_rep = lax.axis_index("rep")
    local_count = pts.shape[0]
    small = n_cl <= 8

    def partner(j):
        return xor(me, j) if small else lax.rem(me + j, n_cl)

    def source(j):
        return xor(me, j) if small else lax.rem(me + n_cl - j, n_cl)

    def each(first, last, body, reverse=False):
        if small:
            for j in range(last - 1, first - 1, -1) if reverse else range(first, last):
                body(j)
        else:
            def step(j, carry):
                body(j)
                return carry
            lax.fori_loop(first, last, step, 0)

    def columns(ref, l):
        return ref.at[:, pl.ds(l * CLUSTER, CLUSTER)]

    in_points = [
        pltpu.make_async_copy(columns(points_hbm, l), pts.at[l], local_sem.at[l])
        for l in range(local_count)]
    in_sketch = [
        pltpu.make_async_copy(columns(sketch_hbm, l), skt.at[l], local_sem.at[local_count + l])
        for l in range(local_count)]
    for copy in in_points + in_sketch:
        copy.start()

    barrier = pltpu.get_barrier_semaphore()
    each(1, n_cl, lambda j: pl.semaphore_signal(
        barrier, inc=1, device_id=(partner(j), my_rep), device_id_type=MESH))
    for j in range(1, n_rep):
        pl.semaphore_signal(barrier, inc=1, device_id=(me, xor(my_rep, j)), device_id_type=MESH)

    for copy in in_points:
        copy.wait()

    def stage_coords(j):
        wanted = send_ids[0, 0, partner(j), 0]
        send_c[j] = pts[wanted]

    def stage_sketch(j):
        wanted = send_ids[0, 0, partner(j), 0]
        send_s[j] = skt[wanted]

    def coords_copy(j):
        return pltpu.make_async_remote_copy(
            src_ref=send_c.at[j], dst_ref=recv_c.at[j], send_sem=csend.at[j], recv_sem=crecv.at[j],
            device_id=(partner(j), my_rep), device_id_type=MESH)

    def sketch_copy(j):
        return pltpu.make_async_remote_copy(
            src_ref=send_s.at[j], dst_ref=recv_s.at[j], send_sem=ssend.at[j], recv_sem=srecv.at[j],
            device_id=(partner(j), my_rep), device_id_type=MESH)

    each(0, n_cl, stage_coords)
    for copy in in_sketch:
        copy.wait()
    each(0, n_cl, stage_sketch)
    pl.semaphore_wait(barrier, n_cl - 1 + n_rep - 1)
    each(1, n_cl, lambda j: coords_copy(j).start(), reverse=True)
    each(1, n_cl, lambda j: sketch_copy(j).start(), reverse=True)

    for l in range(local_count):
        block = pts[l]
        wide = jnp.concatenate([block, jnp.zeros((5, CLUSTER), jnp.float32)], axis=0)
        down = wide.T
        for c in range(3):
            row_b[l, c] = jnp.broadcast_to(down[:, c:c + 1], (CLUSTER, 128))
    acc[...] = jnp.zeros_like(acc)

    def same(a, b):
        return 1 - jnp.minimum((a - b) * (a - b), 1)

    def entry(j):
        slot = source(j)

        def search(i, found):
            hit = same(order[0, 0, i], slot)
            return found[0] + hit * i, found[1] + hit * rows[0, 0, i]

        if small:
            found = (0, 0)
            for i in range(n_cl):
                found = search(i, found)
        else:
            found = lax.fori_loop(0, n_cl, search, (jnp.int32(0), jnp.int32(0)))
        k, row = found
        active = jnp.minimum(jnp.maximum(count[0, 0] - k, 0), 1)
        return row, [(active * same(row, l)).astype(jnp.float32) for l in range(local_count)]

    def evaluate(j, row, col, slot):
        for half in range(CLUSTER // 128):
            lanes = slice(half * 128, (half + 1) * 128)
            squared = None
            for c in range(3):
                differ = row_b[row, c] - col[c:c + 1, lanes]
                squared = differ * differ if squared is None else squared + differ * differ
            inv = lax.rsqrt(squared)
            turns = squared * inv * TURNS
            r = turns - jnp.round(turns)
            u = r * r
            s = horner(SIN_C, u) * r
            c = horner(COS_C, u)
            inv = inv * INV_FOUR_PI
            tile_re[slot, :, lanes] = ((1.0 - s * s) * inv).astype(jnp.bfloat16)
            tile_im[slot, :, lanes] = (s * c * inv).astype(jnp.bfloat16)

    def multiply(factors, weights, slot):
        for e, tile in enumerate((tile_re, tile_im)):
            term = lax.dot_general(
                weights, tile[slot], (((1,), (1,)), ((), ())), preferred_element_type=jnp.float32)
            for l in range(local_count):
                acc[l, e * SK:(e + 1) * SK, :] += term * factors[l]

    row, factors = entry(0)
    evaluate(0, row, send_c[0], 0)
    if small:
        for j in range(1, n_cl):
            new_row, new_factors = entry(j)
            coords_copy(j).wait_recv()
            if j > 1:
                sketch_copy(j - 1).wait_recv()
            evaluate(j, new_row, recv_c[j], j % 2)
            multiply(factors, send_s[0] if j == 1 else recv_s[j - 1], (j - 1) % 2)
            factors = new_factors
        sketch_copy(n_cl - 1).wait_recv()
        multiply(factors, recv_s[n_cl - 1], (n_cl - 1) % 2)
    else:
        multiply(factors, send_s[0], 0)

        def step(j):
            row, factors = entry(j)
            coords_copy(j).wait_recv()
            sketch_copy(j).wait_recv()
            evaluate(j, row, recv_c[j], 0)
            multiply(factors, recv_s[j], 0)
        each(1, n_cl, step)

    def partial_copy(j):
        return pltpu.make_async_remote_copy(
            src_ref=rs_send.at[j - 1], dst_ref=rs_recv.at[j - 1],
            send_sem=rsend.at[j - 1], recv_sem=rrecv.at[j - 1],
            device_id=(me, xor(my_rep, j)), device_id_type=MESH)

    for j in range(n_rep - 1, 0, -1):
        rs_send[j - 1] = acc[xor(my_rep, j)].astype(jnp.bfloat16)
        partial_copy(j).start()
    total = acc[my_rep]
    for j in range(1, n_rep):
        partial_copy(j).wait_recv()
        total = total + rs_recv[j - 1].astype(jnp.float32)
    out_ref[0] = total[:SK]
    out_ref[1] = total[SK:]
    gram_ref[0] = lax.dot_general(
        total, total, (((1,), (1,)), ((), ())),
        preferred_element_type=jnp.float32, precision=lax.Precision.HIGHEST) * (1.0 / CLUSTER)

    each(1, n_cl, lambda j: coords_copy(j).wait_send())
    each(1, n_cl, lambda j: sketch_copy(j).wait_send())
    for j in range(1, n_rep):
        partial_copy(j).wait_send()


def shards(n_cl, n_rep, points, sketch, send_ids, tile_order, tile_rows, tile_count):
    local_count = sketch.shape[1] // CLUSTER
    smem = pl.BlockSpec(memory_space=pltpu.SMEM)
    vmem = pl.BlockSpec(memory_space=pltpu.VMEM)
    hbm = pl.BlockSpec(memory_space=pl.ANY)
    dma = pltpu.SemaphoreType.DMA
    return pl.pallas_call(
        functools.partial(kernel, n_cl, n_rep),
        out_shape=(
            jax.ShapeDtypeStruct((2, SK, CLUSTER), jnp.float32),
            jax.ShapeDtypeStruct((1, 2 * SK, 2 * SK), jnp.float32),
        ),
        in_specs=[smem] * 4 + [hbm] * 2,
        out_specs=(vmem, vmem),
        scratch_shapes=[
            pltpu.VMEM((local_count, 3, CLUSTER), jnp.float32),
            pltpu.VMEM((local_count, SK, CLUSTER), jnp.bfloat16),
            pltpu.VMEM((n_cl, 3, CLUSTER), jnp.float32),
            pltpu.VMEM((n_cl, SK, CLUSTER), jnp.bfloat16),
            pltpu.VMEM((n_cl, 3, CLUSTER), jnp.float32),
            pltpu.VMEM((n_cl, SK, CLUSTER), jnp.bfloat16),
            pltpu.VMEM((local_count, 3, CLUSTER, 128), jnp.float32),
            pltpu.VMEM((2, CLUSTER, CLUSTER), jnp.bfloat16),
            pltpu.VMEM((2, CLUSTER, CLUSTER), jnp.bfloat16),
            pltpu.VMEM((local_count, 2 * SK, CLUSTER), jnp.float32),
            pltpu.VMEM((n_rep - 1, 2 * SK, CLUSTER), jnp.bfloat16),
            pltpu.VMEM((n_rep - 1, 2 * SK, CLUSTER), jnp.bfloat16),
            dma((2 * local_count,)),
            dma((n_cl,)), dma((n_cl,)), dma((n_cl,)), dma((n_cl,)),
            dma((n_rep - 1,)), dma((n_rep - 1,)),
        ],
        compiler_params=pltpu.CompilerParams(
            collective_id=0, has_side_effects=True, vmem_limit_bytes=32 * 2**20
        ),
    )(send_ids, tile_order, tile_rows, tile_count, points, sketch)


def solution(mesh):
    placed = (
        P(None, "cl"),
        P(None, "cl"),
        P("cl", "rep", None, None),
        P("cl", "rep", None),
        P("cl", "rep", None),
        P("cl", "rep"),
    )
    return jax.shard_map(
        functools.partial(shards, mesh.shape["cl"], mesh.shape["rep"]),
        mesh=mesh,
        in_specs=placed,
        out_specs=(P(None, None, ("cl", "rep")), P(("cl", "rep"), None, None)),
        check_vma=False,
    )
```

```python
import functools
import math

import jax
import jax.numpy as jnp
from jax import lax
from jax.experimental import pallas as pl
from jax.experimental.pallas import tpu as pltpu
from jax.sharding import PartitionSpec as P

CLUSTER = 256
SK = 64
WAVENUMBER = 16.0
INV_FOUR_PI = 1.0 / (4.0 * math.pi)
TURNS = WAVENUMBER / (2.0 * math.pi)
MESH = pl.DeviceIdType.MESH

def _fit(fun, terms):
    import numpy as np

    nodes = (np.cos((np.arange(64) + 0.5) * np.pi / 64) + 1.0) / 8.0
    return [float(c) for c in np.polynomial.chebyshev.Chebyshev.fit(
        nodes, fun(np.sqrt(nodes)), terms - 1, domain=[0.0, 0.25]
    ).convert(kind=np.polynomial.Polynomial).coef]


def _coefficients():
    import numpy as np

    root = math.sqrt(2.0)
    return (
        _fit(lambda r: root * np.sin(np.pi * r) / r, 5),
        _fit(lambda r: root * np.cos(np.pi * r), 5),
    )


SIN_C, COS_C = _coefficients()


def horner(coefs, u):
    value = coefs[-1]
    for c in coefs[-2::-1]:
        value = value * u + c
    return value


def xor(index, mask):
    bit, result = 1, index
    while bit <= mask:
        if mask & bit:
            result = result + bit * (1 - 2 * ((index // bit) % 2))
        bit *= 2
    return result


def kernel(
    n_cl, n_rep,
    send_ids_hbm, order_hbm, rows_hbm, count_hbm, points_hbm, sketch_hbm,
    out_ref, gram_ref,
    send_ids, order, rows, count,
    pts, skt, send_c, send_s, recv_c, recv_s, row_b, tile_re, tile_im, acc, rs_send, rs_recv,
    local_sem, csend, crecv, ssend, srecv, rsend, rrecv,
):
    me = lax.axis_index("cl")
    my_rep = lax.axis_index("rep")
    local_count = pts.shape[0]
    small = n_cl <= 8

    def partner(j):
        return xor(me, j) if small else lax.rem(me + j, n_cl)

    def source(j):
        return xor(me, j) if small else lax.rem(me + n_cl - j, n_cl)

    def each(first, last, body, reverse=False):
        if small:
            for j in range(last - 1, first - 1, -1) if reverse else range(first, last):
                body(j)
        else:
            def step(j, carry):
                body(j)
                return carry
            lax.fori_loop(first, last, step, 0)

    def columns(ref, l):
        return ref.at[:, pl.ds(l * CLUSTER, CLUSTER)]

    in_points = [
        pltpu.make_async_copy(columns(points_hbm, l), pts.at[l], local_sem.at[l])
        for l in range(local_count)]
    in_sketch = [
        pltpu.make_async_copy(columns(sketch_hbm, l), skt.at[l], local_sem.at[local_count + l])
        for l in range(local_count)]
    in_lists = [
        pltpu.make_async_copy(src, dst, local_sem.at[2 * local_count + i])
        for i, (src, dst) in enumerate((
            (send_ids_hbm, send_ids), (order_hbm, order), (rows_hbm, rows), (count_hbm, count)))]
    for copy in in_lists + in_points + in_sketch:
        copy.start()

    barrier = pltpu.get_barrier_semaphore()
    each(1, n_cl, lambda j: pl.semaphore_signal(
        barrier, inc=1, device_id=(partner(j), my_rep), device_id_type=MESH))
    for j in range(1, n_rep):
        pl.semaphore_signal(barrier, inc=1, device_id=(me, xor(my_rep, j)), device_id_type=MESH)

    for copy in in_lists + in_points:
        copy.wait()

    def stage_coords(j):
        wanted = send_ids[0, partner(j)]
        send_c[j] = pts[wanted]

    def stage_sketch(j):
        wanted = send_ids[0, partner(j)]
        send_s[j] = skt[wanted]

    def coords_copy(j):
        return pltpu.make_async_remote_copy(
            src_ref=send_c.at[j], dst_ref=recv_c.at[j], send_sem=csend.at[j], recv_sem=crecv.at[j],
            device_id=(partner(j), my_rep), device_id_type=MESH)

    def sketch_copy(j):
        return pltpu.make_async_remote_copy(
            src_ref=send_s.at[j], dst_ref=recv_s.at[j], send_sem=ssend.at[j], recv_sem=srecv.at[j],
            device_id=(partner(j), my_rep), device_id_type=MESH)

    each(0, n_cl, stage_coords)
    for copy in in_sketch:
        copy.wait()
    each(0, n_cl, stage_sketch)
    pl.semaphore_wait(barrier, n_cl - 1 + n_rep - 1)
    each(1, n_cl, lambda j: coords_copy(j).start(), reverse=True)
    each(1, n_cl, lambda j: sketch_copy(j).start(), reverse=True)

    for l in range(local_count):
        block = pts[l]
        wide = jnp.concatenate([block, jnp.zeros((5, CLUSTER), jnp.float32)], axis=0)
        down = wide.T
        for c in range(3):
            row_b[l, c] = jnp.broadcast_to(down[:, c:c + 1], (CLUSTER, 128))
    acc[...] = jnp.zeros_like(acc)

    def same(a, b):
        return 1 - jnp.minimum((a - b) * (a - b), 1)

    def entry(j):
        slot = source(j)

        def search(i, found):
            hit = same(order[0, i], slot)
            return found[0] + hit * i, found[1] + hit * rows[0, i]

        if small:
            found = (0, 0)
            for i in range(n_cl):
                found = search(i, found)
        else:
            found = lax.fori_loop(0, n_cl, search, (jnp.int32(0), jnp.int32(0)))
        k, row = found
        active = jnp.minimum(jnp.maximum(count[0, 0] - k, 0), 1)
        return row, [(active * same(row, l)).astype(jnp.float32) for l in range(local_count)]

    def evaluate(j, row, col, slot):
        for half in range(CLUSTER // 128):
            lanes = slice(half * 128, (half + 1) * 128)
            squared = None
            for c in range(3):
                differ = row_b[row, c] - col[c:c + 1, lanes]
                squared = differ * differ if squared is None else squared + differ * differ
            inv = lax.rsqrt(squared)
            turns = squared * inv * TURNS
            r = turns - jnp.round(turns)
            u = r * r
            s = horner(SIN_C, u) * r
            c = horner(COS_C, u)
            inv = inv * INV_FOUR_PI
            tile_re[slot, :, lanes] = ((1.0 - s * s) * inv).astype(jnp.bfloat16)
            tile_im[slot, :, lanes] = (s * c * inv).astype(jnp.bfloat16)

    def multiply(factors, weights, slot):
        for e, tile in enumerate((tile_re, tile_im)):
            term = lax.dot_general(
                weights, tile[slot], (((1,), (1,)), ((), ())), preferred_element_type=jnp.float32)
            for l in range(local_count):
                acc[l, e * SK:(e + 1) * SK, :] += term * factors[l]

    row, factors = entry(0)
    evaluate(0, row, send_c[0], 0)
    if small:
        for j in range(1, n_cl):
            new_row, new_factors = entry(j)
            coords_copy(j).wait_recv()
            if j > 1:
                sketch_copy(j - 1).wait_recv()
            evaluate(j, new_row, recv_c[j], j % 2)
            multiply(factors, send_s[0] if j == 1 else recv_s[j - 1], (j - 1) % 2)
            factors = new_factors
        sketch_copy(n_cl - 1).wait_recv()
        multiply(factors, recv_s[n_cl - 1], (n_cl - 1) % 2)
    else:
        multiply(factors, send_s[0], 0)

        def step(j):
            row, factors = entry(j)
            coords_copy(j).wait_recv()
            sketch_copy(j).wait_recv()
            evaluate(j, row, recv_c[j], 0)
            multiply(factors, recv_s[j], 0)
        each(1, n_cl, step)

    def partial_copy(j):
        return pltpu.make_async_remote_copy(
            src_ref=rs_send.at[j - 1], dst_ref=rs_recv.at[j - 1],
            send_sem=rsend.at[j - 1], recv_sem=rrecv.at[j - 1],
            device_id=(me, xor(my_rep, j)), device_id_type=MESH)

    for j in range(n_rep - 1, 0, -1):
        rs_send[j - 1] = acc[xor(my_rep, j)].astype(jnp.bfloat16)
        partial_copy(j).start()
    total = acc[my_rep]
    for j in range(1, n_rep):
        partial_copy(j).wait_recv()
        total = total + rs_recv[j - 1].astype(jnp.float32)
    out_ref[0] = total[:SK]
    out_ref[1] = total[SK:]
    gram_ref[0] = lax.dot_general(
        total, total, (((1,), (1,)), ((), ())),
        preferred_element_type=jnp.float32, precision=lax.Precision.HIGHEST) * (1.0 / CLUSTER)

    each(1, n_cl, lambda j: coords_copy(j).wait_send())
    each(1, n_cl, lambda j: sketch_copy(j).wait_send())
    for j in range(1, n_rep):
        partial_copy(j).wait_send()


def shards(n_cl, n_rep, points, sketch, send_ids, tile_order, tile_rows, tile_count):
    local_count = sketch.shape[1] // CLUSTER
    vmem = pl.BlockSpec(memory_space=pltpu.VMEM)
    hbm = pl.BlockSpec(memory_space=pl.ANY)
    dma = pltpu.SemaphoreType.DMA
    return pl.pallas_call(
        functools.partial(kernel, n_cl, n_rep),
        out_shape=(
            jax.ShapeDtypeStruct((2, SK, CLUSTER), jnp.float32),
            jax.ShapeDtypeStruct((1, 2 * SK, 2 * SK), jnp.float32),
        ),
        in_specs=[hbm] * 6,
        out_specs=(vmem, vmem),
        scratch_shapes=[
            pltpu.SMEM((1, n_cl), jnp.int32),
            pltpu.SMEM((1, n_cl), jnp.int32),
            pltpu.SMEM((1, n_cl), jnp.int32),
            pltpu.SMEM((1, 1), jnp.int32),
            pltpu.VMEM((local_count, 3, CLUSTER), jnp.float32),
            pltpu.VMEM((local_count, SK, CLUSTER), jnp.bfloat16),
            pltpu.VMEM((n_cl, 3, CLUSTER), jnp.float32),
            pltpu.VMEM((n_cl, SK, CLUSTER), jnp.bfloat16),
            pltpu.VMEM((n_cl, 3, CLUSTER), jnp.float32),
            pltpu.VMEM((n_cl, SK, CLUSTER), jnp.bfloat16),
            pltpu.VMEM((local_count, 3, CLUSTER, 128), jnp.float32),
            pltpu.VMEM((2, CLUSTER, CLUSTER), jnp.bfloat16),
            pltpu.VMEM((2, CLUSTER, CLUSTER), jnp.bfloat16),
            pltpu.VMEM((local_count, 2 * SK, CLUSTER), jnp.float32),
            pltpu.VMEM((n_rep - 1, 2 * SK, CLUSTER), jnp.bfloat16),
            pltpu.VMEM((n_rep - 1, 2 * SK, CLUSTER), jnp.bfloat16),
            dma((2 * local_count + 4,)),
            dma((n_cl,)), dma((n_cl,)), dma((n_cl,)), dma((n_cl,)),
            dma((n_rep - 1,)), dma((n_rep - 1,)),
        ],
        compiler_params=pltpu.CompilerParams(
            collective_id=0, has_side_effects=True, vmem_limit_bytes=60 * 2**20
        ),
    )(
        send_ids.reshape(1, n_cl), tile_order.reshape(1, n_cl), tile_rows.reshape(1, n_cl),
        tile_count, points, sketch)


def solution(mesh):
    placed = (
        P(None, "cl"),
        P(None, "cl"),
        P("cl", "rep", None, None),
        P("cl", "rep", None),
        P("cl", "rep", None),
        P("cl", "rep"),
    )
    return jax.shard_map(
        functools.partial(shards, mesh.shape["cl"], mesh.shape["rep"]),
        mesh=mesh,
        in_specs=placed,
        out_specs=(P(None, None, ("cl", "rep")), P(("cl", "rep"), None, None)),
        check_vma=False,
    )
```
